32 devices in a mesh: groups: 2 (over y), dp: 8 (over z, x), tensor: 2 (over core).
Axes of the slice: x: 2, y: 2, z: 4, core: 2. Of those that a mesh axis runs over, the one named last changes fastest.
Arguments:
- cache_keys: bfloat16 [16, 2048, 1024], P(('groups', 'dp'), None, 'tensor'), parts along dimension 0, may hold values from -32 to 32
- cache_values: bfloat16 [16, 2048, 1024], P(('groups', 'dp'), None, 'tensor'), parts along dimension 0, may hold values from -6 to 6
- lengths: int32 [16], P(('groups', 'dp')), parts along dimension 0, may hold values from 512 to 2048
- parent_scores: float32 [16], P(('groups', 'dp')), parts along dimension 0, may hold values from -6 to 0
- parents: int32 [16], P(('groups', 'dp')), parts along dimension 0, may hold values from 0 to 7, as said below
- queries: bfloat16 [16, 4, 8192], P(('groups', 'dp'), None, 'tensor'), parts along dimension 0, may hold values from -32 to 32
- new_keys: bfloat16 [16, 4, 1024], P(('groups', 'dp'), None, 'tensor'), parts along dimension 0, may hold values from -9 to 9
- new_values: bfloat16 [16, 4, 1024], P(('groups', 'dp'), None, 'tensor'), parts along dimension 0, may hold values from -6 to 6
- reward_weight: bfloat16 [8192], P('tensor'), may hold values from -3 to 3
Outputs:
- attended: bfloat16 [16, 4, 8192], P(('groups', 'dp'), None, 'tensor'), parts along dimension 0
- scores: float32 [16], P(('groups', 'dp')), parts along dimension 0
The draws below stay inside these ranges and needn't reach their ends.
There are 2 independent parts, one for each index of `groups`. The reference program is written for one: setup_inputs(seed, part) draws one part's arguments, and reference() takes and returns one part's arrays. A program takes and returns all parts, laid end to end along the dimension named above; an argument that names none is the same for every part. Nothing has to cross between parts.
Inputs may be any that keep to these rules, and one draw needn't show every extreme that they name: `parents`: each old beam is continued by at most 2 new slots; in every draw some old beams are continued by exactly 2 and others by none.
All inputs are finite; a program needn't handle non-finite values.
Results may differ from the reference program's by a relative error of at most 0.0056.
Values may be sent and summed in bfloat16 or wider, within the bound.
A program may use at most 64 MiB of HBM per device.

```python
import jax
import jax.numpy as jnp
from jax import lax

QH = 64
KVH = 8
HD = 128
CTX = 2048
STEPS = 4
BEAMS = 8


def parent_table(key):
    base = jax.random.fold_in(key, 7001)
    key_order, key_shuffle = jax.random.split(base, 2)
    order = jax.random.permutation(key_order, BEAMS)
    ranked = jnp.arange(BEAMS)
    by_rank = jnp.where(ranked < BEAMS // 4, 2, jnp.where(ranked < 3 * (BEAMS // 4), 1, 0)).astype(jnp.int32)
    counts = jnp.zeros((BEAMS,), jnp.int32).at[order].set(by_rank)
    listed = jnp.repeat(jnp.arange(BEAMS, dtype=jnp.int32), counts, total_repeat_length=BEAMS)
    shuffle = jax.random.permutation(key_shuffle, BEAMS)
    listed = listed[shuffle].astype(jnp.int32)
    first = listed[0]
    target = ((first + BEAMS // 2) % BEAMS).astype(jnp.int32)
    other = listed[target]
    listed = listed.at[0].set(other)
    listed = listed.at[target].set(first)
    return listed.astype(jnp.int32)


def draw_parents(key, part):
    return parent_table(key)


def draw_cache_keys(key, part):
    base = jax.random.normal(jax.random.fold_in(key, 7003), (BEAMS, CTX, KVH, HD), jnp.float32)
    base = jnp.clip(base, -32.0, 32.0)
    return base.reshape(BEAMS, CTX, KVH * HD).astype(jnp.bfloat16)


def draw_queries(key, part):
    base = jax.random.normal(jax.random.fold_in(key, 7004), (BEAMS, STEPS, QH, HD), jnp.float32)
    base = jnp.clip(base, -32.0, 32.0)
    return base.reshape(BEAMS, STEPS, QH * HD).astype(jnp.bfloat16)


def with_ends(result, stream_key, least, high):
    dims = result.shape
    index_at = [jax.random.randint(jax.random.fold_in(stream_key, axis), (), 0, dims[axis]) for axis in range(len(dims))]
    result = result.at[tuple(index_at)].set(least)
    longest = dims.index(max(dims))
    index_at[longest] = (index_at[longest] + 1) % dims[longest]
    return result.at[tuple(index_at)].set(high)


def shard_levels(own_key, dims, cuts, low, largest):
    def one(axis_at, blocks):
        heights = jax.random.uniform(jax.random.fold_in(jax.random.fold_in(own_key, 6), axis_at), (blocks,), jnp.float32, low / len(cuts), largest / len(cuts))
        return jnp.repeat(jnp.exp(heights), dims[axis_at] // blocks).reshape((-1,) + (1,) * (len(dims) - axis_at - 1))

    gain = one(*cuts[0])
    for cut in cuts[1:]:
        gain = gain * one(*cut)
    return gain


def noise(stream_key, dims, scale, reach, cuts=(), kind=jnp.bfloat16):
    values = scale * jax.random.normal(stream_key, dims, jnp.float32)
    if cuts:
        values = values * shard_levels(stream_key, dims, cuts, -0.22, 0.18)
    return jnp.clip(values, -reach, reach).astype(kind)


def setup_inputs(seed: int = 0, part: int = 0) -> dict:
    key_list = jax.random.split(jax.random.key(seed), 10)
    part_keys = jax.random.split(jax.random.fold_in(key_list[9], part), 10)
    cache_keys = draw_cache_keys(jax.random.fold_in(jax.random.fold_in(key_list[9], part), 71), part)
    cache_values = noise(part_keys[1], (BEAMS, CTX, KVH * HD), 1.0, 6.0, ((0, 8), (2, 2)))
    lengths = with_ends(jax.random.randint(part_keys[2], (BEAMS,), CTX // 4, CTX + 1), jax.random.fold_in(part_keys[2], 1), CTX // 4, CTX).astype(jnp.int32)
    parent_scores = jnp.clip(-6.0 + 6.0 * jax.random.uniform(part_keys[3], (BEAMS,), jnp.float32) ** shard_levels(part_keys[3], (BEAMS,), ((0, 8),), -0.2, 0.2), -6.0, 0.0)
    parents = draw_parents(jax.random.fold_in(jax.random.fold_in(key_list[9], part), 71), part)
    queries = draw_queries(jax.random.fold_in(jax.random.fold_in(key_list[9], part), 71), part)
    new_keys = noise(part_keys[6], (BEAMS, STEPS, KVH * HD), 1.5, 9.0, ((0, 8), (2, 2)))
    new_values = noise(part_keys[7], (BEAMS, STEPS, KVH * HD), 1.0, 6.0, ((0, 8), (2, 2)))
    reward_weight = noise(key_list[8], (QH * HD,), 0.5, 3.0, ((0, 2),))
    return dict(cache_keys=cache_keys, cache_values=cache_values, lengths=lengths, parent_scores=parent_scores, parents=parents, queries=queries, new_keys=new_keys, new_values=new_values, reward_weight=reward_weight)


def reference(cache_keys, cache_values, lengths, parent_scores, parents, queries, new_keys, new_values, reward_weight):
    group = QH // KVH
    scale = HD ** -0.5
    positions = jnp.arange(CTX)
    causal = jnp.arange(STEPS)[None, :] <= jnp.arange(STEPS)[:, None]

    def one_slot(index):
        parent = parents[index]
        keys = cache_keys[parent].astype(jnp.float32).reshape(CTX, KVH, HD)
        values = cache_values[parent].astype(jnp.float32).reshape(CTX, KVH, HD)
        query = queries[index].astype(jnp.float32).reshape(STEPS, KVH, group, HD)
        logits = jnp.einsum('tgjd,cgd->tgjc', query, keys) * scale
        valid = positions < lengths[parent]
        logits = jnp.where(valid[None, None, None, :], logits, -1e30)
        top_parent = jnp.max(logits, axis=-1)
        weights = jnp.exp(logits - top_parent[..., None])
        total_parent = jnp.sum(weights, axis=-1)
        rounded = weights.astype(jnp.bfloat16).astype(jnp.float32)
        sum_parent = jnp.einsum('tgjc,cgd->tgjd', rounded, values)
        parent_out = (sum_parent / total_parent[..., None]).astype(jnp.bfloat16).astype(jnp.float32)
        parent_lse = top_parent + jnp.log(total_parent)
        own_keys = new_keys[index].astype(jnp.float32).reshape(STEPS, KVH, HD)
        own_values = new_values[index].astype(jnp.float32).reshape(STEPS, KVH, HD)
        own_logits = jnp.einsum('tgjd,ugd->tgju', query, own_keys) * scale
        own_logits = jnp.where(causal[:, None, None, :], own_logits, -1e30)
        top_own = jnp.max(own_logits, axis=-1)
        own_weights = jnp.exp(own_logits - top_own[..., None])
        total_own = jnp.sum(own_weights, axis=-1)
        own_rounded = own_weights.astype(jnp.bfloat16).astype(jnp.float32)
        sum_own = jnp.einsum('tgju,ugd->tgjd', own_rounded, own_values)
        top = jnp.maximum(parent_lse, top_own)
        factor_parent = jnp.exp(parent_lse - top)
        factor_own = jnp.exp(top_own - top)
        merged = (parent_out * factor_parent[..., None] + sum_own * factor_own[..., None]) / (factor_parent + total_own * factor_own)[..., None]
        output = merged.reshape(STEPS, QH * HD).astype(jnp.bfloat16)
        reward = jnp.dot(output, reward_weight, preferred_element_type=jnp.float32)
        score = parent_scores[parent] + jnp.sum(jax.nn.log_sigmoid(reward))
        return output, score

    attended, scores = lax.map(one_slot, jnp.arange(BEAMS))
    return attended, scores
```

```python
import functools
import math

import jax
import jax.numpy as jnp
from jax import lax
from jax.experimental import pallas as pl
from jax.experimental.pallas import tpu as pltpu
from jax.sharding import PartitionSpec as P

HD = 128
MESH = pl.DeviceIdType.MESH
F32 = jnp.float32
BF16 = jnp.bfloat16


def kernel(
    n,
    lengths,
    parent_scores,
    parents,
    queries,
    new_keys,
    new_values,
    reward_weight,
    cache_keys,
    cache_values,
    attended,
    scores,
    keys,
    values,
    stage,
    weight,
    ids,
    asked,
    answer,
    answer_lse,
    got,
    got_lse,
    part,
    cache_sems,
    id_sems,
    ask_sems,
    got_sems,
    lse_sems,
    part_sems,
):
    me = lax.axis_index("dp")
    core = lax.axis_index("tensor")
    steps = queries.shape[1]
    heads = queries.shape[2] // HD
    context = cache_keys.shape[1]
    kv_heads = cache_keys.shape[2] // HD
    group = heads // kv_heads
    rows = group * steps
    total_rows = heads * steps
    scale = HD ** (-0.5)
    base2 = scale * math.log2(math.e)

    copy_keys = pltpu.make_async_copy(cache_keys.at[0], keys, cache_sems.at[0])
    copy_values = pltpu.make_async_copy(cache_values.at[0], values, cache_sems.at[1])
    copy_keys.start()
    copy_values.start()

    barrier = pltpu.get_barrier_semaphore()

    def peer(k):
        return lax.rem(me + 1 + k, n)

    def greet(k, carry):
        pl.semaphore_signal(barrier, inc=1, device_id={"dp": peer(k)}, device_id_type=MESH)
        return carry

    lax.fori_loop(0, n - 1, greet, 0)
    pl.semaphore_signal(barrier, inc=1, device_id={"tensor": 1 - core}, device_id_type=MESH)

    for head in range(heads):
        stage[head * steps : (head + 1) * steps, :] = queries[
            0, :, head * HD : (head + 1) * HD
        ].astype(F32)
        weight[head * steps : (head + 1) * steps, :] = jnp.broadcast_to(
            reward_weight[:, head * HD : (head + 1) * HD].astype(F32), (steps, HD)
        )
    query = stage[...].astype(BF16)
    asked[me] = query
    ids[me] = jnp.full((8, HD), parents[0], jnp.int32)

    pl.semaphore_wait(barrier, n)

    def ask_copy(slot, to):
        return pltpu.make_async_remote_copy(
            src_ref=asked.at[slot],
            dst_ref=asked.at[slot],
            send_sem=ask_sems.at[0, to],
            recv_sem=ask_sems.at[1, slot],
            device_id={"dp": to},
            device_id_type=MESH,
        )

    def id_copy(slot, to):
        return pltpu.make_async_remote_copy(
            src_ref=ids.at[slot],
            dst_ref=ids.at[slot],
            send_sem=id_sems.at[0, to],
            recv_sem=id_sems.at[1, slot],
            device_id={"dp": to},
            device_id_type=MESH,
        )

    def got_copy(slot, to):
        return pltpu.make_async_remote_copy(
            src_ref=answer.at[to],
            dst_ref=got.at[slot],
            send_sem=got_sems.at[0, to],
            recv_sem=got_sems.at[1, slot],
            device_id={"dp": to},
            device_id_type=MESH,
        )

    def lse_copy(slot, to):
        return pltpu.make_async_remote_copy(
            src_ref=answer_lse.at[to],
            dst_ref=got_lse.at[slot],
            send_sem=lse_sems.at[0, to],
            recv_sem=lse_sems.at[1, slot],
            device_id={"dp": to},
            device_id_type=MESH,
        )

    def ask(k, carry):
        id_copy(me, peer(k)).start()
        ask_copy(me, peer(k)).start()
        return carry

    lax.fori_loop(0, n - 1, ask, 0)

    own_keys = new_keys[0]
    own_values = new_values[0]
    row_step = lax.rem(lax.broadcasted_iota(jnp.int32, (rows, steps), 0), steps)
    causal = lax.broadcasted_iota(jnp.int32, (rows, steps), 1) <= row_step
    own_sums, own_tops, own_totals = [], [], []
    for head in range(kv_heads):
        q = query[head * rows : (head + 1) * rows]
        logits = lax.dot_general(
            q,
            own_keys[:, head * HD : (head + 1) * HD],
            (((1,), (1,)), ((), ())),
            preferred_element_type=F32,
        )
        logits = jnp.where(causal, logits * scale, -1e30)
        top = jnp.max(logits, axis=1, keepdims=True)
        weights = jnp.exp(logits - top)
        own_tops.append(top)
        own_totals.append(jnp.sum(weights, axis=1, keepdims=True))
        own_sums.append(
            jnp.dot(
                weights.astype(BF16),
                own_values[:, head * HD : (head + 1) * HD],
                preferred_element_type=F32,
            )
        )
    top_own = jnp.concatenate(own_tops, axis=0)
    total_own = jnp.concatenate(own_totals, axis=0)
    sum_own = jnp.concatenate(own_sums, axis=0)

    copy_keys.wait()
    copy_values.wait()

    def asked_wait(k, carry):
        id_copy(peer(k), me).wait_recv()
        ask_copy(peer(k), me).wait_recv()
        return carry

    lax.fori_loop(0, n - 1, asked_wait, 0)

    def find(slot, carry):
        first, last = carry
        mine = ids[slot] == me
        return (
            jnp.minimum(first, jnp.where(mine, slot, n)),
            jnp.maximum(last, jnp.where(mine, slot, -1)),
        )

    first, last = lax.fori_loop(
        0, n, find, (jnp.full((8, HD), n, jnp.int32), jnp.full((8, HD), -1, jnp.int32))
    )
    first = jnp.minimum(jnp.max(first), n - 1)
    last = jnp.maximum(jnp.max(last), 0)
    both = (asked[first], asked[last])

    valid = lax.broadcasted_iota(jnp.int32, (2 * rows, context), 1) < lengths[0]
    outs, lses = ([], []), ([], [])
    for head in range(kv_heads):
        q = jnp.concatenate([b[head * rows : (head + 1) * rows] for b in both], axis=0)
        logits = lax.dot_general(
            q,
            keys[:, head * HD : (head + 1) * HD],
            (((1,), (1,)), ((), ())),
            preferred_element_type=F32,
        )
        logits = jnp.where(valid, logits, -1e30)
        top = jnp.max(logits, axis=1, keepdims=True)
        weights = jnp.exp2((logits - top) * base2)
        total = jnp.sum(weights, axis=1, keepdims=True)
        summed = jnp.dot(
            weights.astype(BF16),
            values[:, head * HD : (head + 1) * HD],
            preferred_element_type=F32,
        )
        out = (summed / total).astype(BF16)
        lse = top * scale + jnp.log(total)
        for child in range(2):
            outs[child].append(out[child * rows : (child + 1) * rows])
            lses[child].append(lse[child * rows : (child + 1) * rows])

    eye = lax.broadcasted_iota(jnp.int32, (total_rows, total_rows), 0) == lax.broadcasted_iota(
        jnp.int32, (total_rows, total_rows), 1
    )
    out_by_child = [jnp.concatenate(o, axis=0) for o in outs]
    lse_by_child = [
        jnp.sum(jnp.where(eye, jnp.concatenate(l, axis=0), 0.0), axis=0, keepdims=True)
        for l in lses
    ]
    score_row = jnp.full((1, total_rows), parent_scores[0], F32)

    def reply(k, carry):
        to = peer(k)
        answer[to] = jnp.where(to == first, out_by_child[0], out_by_child[1])
        answer_lse[to, 0:1, :] = jnp.where(to == first, lse_by_child[0], lse_by_child[1])
        answer_lse[to, 1:2, :] = score_row
        got_copy(me, to).start()
        lse_copy(me, to).start()
        return carry

    lax.fori_loop(0, n - 1, reply, 0)
    got[me] = jnp.where(me == first, out_by_child[0], out_by_child[1])
    got_lse[me, 0:1, :] = jnp.where(me == first, lse_by_child[0], lse_by_child[1])
    got_lse[me, 1:2, :] = score_row

    def reply_wait(k, carry):
        got_copy(peer(k), me).wait_recv()
        lse_copy(peer(k), me).wait_recv()
        return carry

    lax.fori_loop(0, n - 1, reply_wait, 0)

    holder = parents[0]
    parent_out = got[holder].astype(F32)
    lse_rows = got_lse[holder]
    inherited = jnp.max(lse_rows[1:2, :])
    parent_lse = jnp.sum(jnp.where(eye, lse_rows[0:1, :], 0.0), axis=1, keepdims=True)
    top = jnp.maximum(parent_lse, top_own)
    factor_parent = jnp.exp(parent_lse - top)
    factor_own = jnp.exp(top_own - top)
    merged = (parent_out * factor_parent + sum_own * factor_own) / (
        factor_parent + total_own * factor_own
    )
    output = merged.astype(BF16).astype(F32)
    stage[...] = output
    product = output * weight[...]
    tall = 2 * steps
    partial = product[0:tall]
    for i in range(1, total_rows // tall):
        partial = partial + product[i * tall : (i + 1) * tall]
    part[0] = partial
    part_copy = pltpu.make_async_remote_copy(
        src_ref=part.at[0],
        dst_ref=part.at[1],
        send_sem=part_sems.at[0],
        recv_sem=part_sems.at[1],
        device_id={"tensor": 1 - core},
        device_id_type=MESH,
    )
    part_copy.start()
    for head in range(heads):
        attended[0, :, head * HD : (head + 1) * HD] = stage[
            head * steps : (head + 1) * steps, :
        ].astype(BF16)

    def sent_wait(k, carry):
        id_copy(me, peer(k)).wait_send()
        ask_copy(me, peer(k)).wait_send()
        got_copy(me, peer(k)).wait_send()
        lse_copy(me, peer(k)).wait_send()
        return carry

    lax.fori_loop(0, n - 1, sent_wait, 0)
    part_copy.wait()
    reward = jnp.sum(part[0] + part[1], axis=1, keepdims=True)
    reward = reward[0:steps] + reward[steps : 2 * steps]
    logs = jnp.minimum(reward, 0.0) - jnp.log1p(jnp.exp(-jnp.abs(reward)))
    scores[0] = inherited + jnp.sum(logs)


def per_device(
    n,
    cache_keys,
    cache_values,
    lengths,
    parent_scores,
    parents,
    queries,
    new_keys,
    new_values,
    reward_weight,
):
    steps = queries.shape[1]
    width = queries.shape[2]
    context, kv_width = cache_keys.shape[1:]
    total_rows = steps * width // HD
    vmem = pl.BlockSpec(memory_space=pltpu.VMEM)
    smem = pl.BlockSpec(memory_space=pltpu.SMEM)
    hbm = pl.BlockSpec(memory_space=pl.ANY)
    return pl.pallas_call(
        functools.partial(kernel, n),
        out_shape=(
            jax.ShapeDtypeStruct(queries.shape, BF16),
            jax.ShapeDtypeStruct((1,), F32),
        ),
        in_specs=[smem] * 3 + [vmem] * 4 + [hbm] * 2,
        out_specs=(vmem, smem),
        scratch_shapes=[
            pltpu.VMEM((context, kv_width), BF16),
            pltpu.VMEM((context, kv_width), BF16),
            pltpu.VMEM((total_rows, HD), F32),
            pltpu.VMEM((total_rows, HD), F32),
            pltpu.VMEM((n, 8, HD), jnp.int32),
            pltpu.VMEM((n, total_rows, HD), BF16),
            pltpu.VMEM((n, total_rows, HD), BF16),
            pltpu.VMEM((n, 8, total_rows), F32),
            pltpu.VMEM((n, total_rows, HD), BF16),
            pltpu.VMEM((n, 8, total_rows), F32),
            pltpu.VMEM((2, 2 * steps, HD), F32),
            pltpu.SemaphoreType.DMA((2,)),
            pltpu.SemaphoreType.DMA((2, n)),
            pltpu.SemaphoreType.DMA((2, n)),
            pltpu.SemaphoreType.DMA((2, n)),
            pltpu.SemaphoreType.DMA((2, n)),
            pltpu.SemaphoreType.DMA((2,)),
        ],
        compiler_params=pltpu.CompilerParams(
            collective_id=0, has_side_effects=True, vmem_limit_bytes=48 * 1024 * 1024
        ),
    )(
        lengths,
        parent_scores,
        parents,
        queries,
        new_keys,
        new_values,
        reward_weight.reshape(1, width),
        cache_keys,
        cache_values,
    )


def solution(mesh):
    beams = P(("groups", "dp"))
    split = P(("groups", "dp"), None, "tensor")
    return jax.shard_map(
        functools.partial(per_device, mesh.shape["dp"]),
        mesh=mesh,
        in_specs=(split, split, beams, beams, beams, split, split, split, P("tensor")),
        out_specs=(split, beams),
        check_vma=False,
    )
```

```python
import functools
import math

import jax
import jax.numpy as jnp
from jax import lax
from jax.experimental import pallas as pl
from jax.experimental.pallas import tpu as pltpu
from jax.sharding import PartitionSpec as P

HD = 128
MESH = pl.DeviceIdType.MESH
F32 = jnp.float32
BF16 = jnp.bfloat16


def kernel(
    n,
    lengths_in,
    parent_scores_in,
    parents_in,
    queries_in,
    new_keys_in,
    new_values_in,
    reward_weight_in,
    cache_keys,
    cache_values,
    attended,
    scores,
    lengths,
    parent_scores,
    parents,
    queries,
    new_keys,
    new_values,
    reward_weight,
    keys,
    values,
    stage,
    weight,
    ids,
    asked,
    answer,
    answer_lse,
    got,
    got_lse,
    part,
    small_sems,
    cache_sems,
    id_sems,
    ask_sems,
    got_sems,
    lse_sems,
    part_sems,
):
    me = lax.axis_index("dp")
    core = lax.axis_index("tensor")
    steps = queries.shape[1]
    heads = queries.shape[2] // HD
    context = cache_keys.shape[1]
    kv_heads = cache_keys.shape[2] // HD
    group = heads // kv_heads
    rows = group * steps
    total_rows = heads * steps
    scale = HD ** (-0.5)
    base2 = scale * math.log2(math.e)

    small = [
        pltpu.make_async_copy(source, target, small_sems.at[i])
        for i, (source, target) in enumerate(
            (
                (queries_in, queries),
                (parents_in, parents),
                (new_keys_in, new_keys),
                (new_values_in, new_values),
                (reward_weight_in, reward_weight),
                (lengths_in, lengths),
                (parent_scores_in, parent_scores),
            )
        )
    ]
    for copy in small:
        copy.start()
    copy_keys = pltpu.make_async_copy(cache_keys.at[0], keys, cache_sems.at[0])
    copy_values = pltpu.make_async_copy(cache_values.at[0], values, cache_sems.at[1])
    copy_keys.start()
    copy_values.start()

    barrier = pltpu.get_barrier_semaphore()

    def peer(k):
        return lax.rem(me + 1 + k, n)

    def greet(k, carry):
        pl.semaphore_signal(barrier, inc=1, device_id={"dp": peer(k)}, device_id_type=MESH)
        return carry

    lax.fori_loop(0, n - 1, greet, 0)
    pl.semaphore_signal(barrier, inc=1, device_id={"tensor": 1 - core}, device_id_type=MESH)

    small[0].wait()
    small[1].wait()
    for head in range(heads):
        stage[head * steps : (head + 1) * steps, :] = queries[
            0, :, head * HD : (head + 1) * HD
        ].astype(F32)
    query = stage[...].astype(BF16)
    asked[me] = query
    ids[me] = jnp.full((8, HD), parents[0], jnp.int32)

    pl.semaphore_wait(barrier, n)

    def ask_copy(slot, to):
        return pltpu.make_async_remote_copy(
            src_ref=asked.at[slot],
            dst_ref=asked.at[slot],
            send_sem=ask_sems.at[0, to],
            recv_sem=ask_sems.at[1, slot],
            device_id={"dp": to},
            device_id_type=MESH,
        )

    def id_copy(slot, to):
        return pltpu.make_async_remote_copy(
            src_ref=ids.at[slot],
            dst_ref=ids.at[slot],
            send_sem=id_sems.at[0, to],
            recv_sem=id_sems.at[1, slot],
            device_id={"dp": to},
            device_id_type=MESH,
        )

    def got_copy(slot, to):
        return pltpu.make_async_remote_copy(
            src_ref=answer.at[to],
            dst_ref=got.at[slot],
            send_sem=got_sems.at[0, to],
            recv_sem=got_sems.at[1, slot],
            device_id={"dp": to},
            device_id_type=MESH,
        )

    def lse_copy(slot, to):
        return pltpu.make_async_remote_copy(
            src_ref=answer_lse.at[to],
            dst_ref=got_lse.at[slot],
            send_sem=lse_sems.at[0, to],
            recv_sem=lse_sems.at[1, slot],
            device_id={"dp": to},
            device_id_type=MESH,
        )

    def ask(k, carry):
        id_copy(me, peer(k)).start()
        ask_copy(me, peer(k)).start()
        return carry

    lax.fori_loop(0, n - 1, ask, 0)

    for copy in small[2:]:
        copy.wait()
    for head in range(heads):
        weight[head * steps : (head + 1) * steps, :] = jnp.broadcast_to(
            reward_weight[head * HD : (head + 1) * HD].astype(F32)[None], (steps, HD)
        )

    own_keys = new_keys[0]
    own_values = new_values[0]
    row_step = lax.rem(lax.broadcasted_iota(jnp.int32, (rows, steps), 0), steps)
    causal = lax.broadcasted_iota(jnp.int32, (rows, steps), 1) <= row_step
    own_sums, own_tops, own_totals = [], [], []
    for head in range(kv_heads):
        q = query[head * rows : (head + 1) * rows]
        logits = lax.dot_general(
            q,
            own_keys[:, head * HD : (head + 1) * HD],
            (((1,), (1,)), ((), ())),
            preferred_element_type=F32,
        )
        logits = jnp.where(causal, logits * scale, -1e30)
        top = jnp.max(logits, axis=1, keepdims=True)
        weights = jnp.exp(logits - top)
        own_tops.append(top)
        own_totals.append(jnp.sum(weights, axis=1, keepdims=True))
        own_sums.append(
            jnp.dot(
                weights.astype(BF16),
                own_values[:, head * HD : (head + 1) * HD],
                preferred_element_type=F32,
            )
        )
    top_own = jnp.concatenate(own_tops, axis=0)
    total_own = jnp.concatenate(own_totals, axis=0)
    sum_own = jnp.concatenate(own_sums, axis=0)

    copy_keys.wait()
    copy_values.wait()

    def asked_wait(k, carry):
        id_copy(peer(k), me).wait_recv()
        ask_copy(peer(k), me).wait_recv()
        return carry

    lax.fori_loop(0, n - 1, asked_wait, 0)

    def find(slot, carry):
        first, last = carry
        mine = ids[slot] == me
        return (
            jnp.minimum(first, jnp.where(mine, slot, n)),
            jnp.maximum(last, jnp.where(mine, slot, -1)),
        )

    first, last = lax.fori_loop(
        0, n, find, (jnp.full((8, HD), n, jnp.int32), jnp.full((8, HD), -1, jnp.int32))
    )
    first = jnp.minimum(jnp.max(first), n - 1)
    last = jnp.maximum(jnp.max(last), 0)
    both = (asked[first], asked[last])

    place = lax.broadcasted_iota(jnp.int32, (1, context), 1)
    bias = jnp.where(place < lengths[0], 0.0, -1e30)
    outs, lses = ([], []), ([], [])
    for head in range(kv_heads):
        q = jnp.concatenate([b[head * rows : (head + 1) * rows] for b in both], axis=0)
        logits = lax.dot_general(
            q,
            keys[:, head * HD : (head + 1) * HD],
            (((1,), (1,)), ((), ())),
            preferred_element_type=F32,
        )
        logits = logits + bias
        top = jnp.max(logits, axis=1, keepdims=True)
        weights = jnp.exp2((logits - top) * base2)
        total = jnp.sum(weights, axis=1, keepdims=True)
        summed = jnp.dot(
            weights.astype(BF16),
            values[:, head * HD : (head + 1) * HD],
            preferred_element_type=F32,
        )
        out = (summed / total).astype(BF16)
        lse = top * scale + jnp.log(total)
        for child in range(2):
            outs[child].append(out[child * rows : (child + 1) * rows])
            lses[child].append(lse[child * rows : (child + 1) * rows])

    eye = lax.broadcasted_iota(jnp.int32, (total_rows, total_rows), 0) == lax.broadcasted_iota(
        jnp.int32, (total_rows, total_rows), 1
    )
    out_by_child = [jnp.concatenate(o, axis=0) for o in outs]
    lse_by_child = [
        jnp.sum(jnp.where(eye, jnp.concatenate(l, axis=0), 0.0), axis=0, keepdims=True)
        for l in lses
    ]
    score_row = jnp.full((1, total_rows), parent_scores[0], F32)

    def reply(k, carry):
        to = peer(k)
        answer[to] = jnp.where(to == first, out_by_child[0], out_by_child[1])
        answer_lse[to, 0:1, :] = jnp.where(to == first, lse_by_child[0], lse_by_child[1])
        answer_lse[to, 1:2, :] = score_row
        got_copy(me, to).start()
        lse_copy(me, to).start()
        return carry

    lax.fori_loop(0, n - 1, reply, 0)
    got[me] = jnp.where(me == first, out_by_child[0], out_by_child[1])
    got_lse[me, 0:1, :] = jnp.where(me == first, lse_by_child[0], lse_by_child[1])
    got_lse[me, 1:2, :] = score_row

    def reply_wait(k, carry):
        got_copy(peer(k), me).wait_recv()
        lse_copy(peer(k), me).wait_recv()
        return carry

    lax.fori_loop(0, n - 1, reply_wait, 0)

    holder = parents[0]
    parent_out = got[holder].astype(F32)
    lse_rows = got_lse[holder]
    inherited = jnp.max(lse_rows[1:2, :])
    parent_lse = jnp.sum(jnp.where(eye, lse_rows[0:1, :], 0.0), axis=1, keepdims=True)
    top = jnp.maximum(parent_lse, top_own)
    factor_parent = jnp.exp(parent_lse - top)
    factor_own = jnp.exp(top_own - top)
    merged = (parent_out * factor_parent + sum_own * factor_own) / (
        factor_parent + total_own * factor_own
    )
    output = merged.astype(BF16).astype(F32)
    stage[...] = output
    product = output * weight[...]
    tall = 2 * steps
    partial = product[0:tall]
    for i in range(1, total_rows // tall):
        partial = partial + product[i * tall : (i + 1) * tall]
    part[0] = partial
    part_copy = pltpu.make_async_remote_copy(
        src_ref=part.at[0],
        dst_ref=part.at[1],
        send_sem=part_sems.at[0],
        recv_sem=part_sems.at[1],
        device_id={"tensor": 1 - core},
        device_id_type=MESH,
    )
    part_copy.start()
    for head in range(heads):
        attended[0, :, head * HD : (head + 1) * HD] = stage[
            head * steps : (head + 1) * steps, :
        ].astype(BF16)

    def sent_wait(k, carry):
        id_copy(me, peer(k)).wait_send()
        ask_copy(me, peer(k)).wait_send()
        got_copy(me, peer(k)).wait_send()
        lse_copy(me, peer(k)).wait_send()
        return carry

    lax.fori_loop(0, n - 1, sent_wait, 0)
    part_copy.wait()
    reward = jnp.sum(part[0] + part[1], axis=1, keepdims=True)
    reward = reward[0:steps] + reward[steps : 2 * steps]
    logs = jnp.minimum(reward, 0.0) - jnp.log1p(jnp.exp(-jnp.abs(reward)))
    scores[0] = inherited + jnp.sum(logs)


def per_device(
    n,
    cache_keys,
    cache_values,
    lengths,
    parent_scores,
    parents,
    queries,
    new_keys,
    new_values,
    reward_weight,
):
    steps = queries.shape[1]
    width = queries.shape[2]
    context, kv_width = cache_keys.shape[1:]
    total_rows = steps * width // HD
    vmem = pl.BlockSpec(memory_space=pltpu.VMEM)
    smem = pl.BlockSpec(memory_space=pltpu.SMEM)
    return pl.pallas_call(
        functools.partial(kernel, n),
        out_shape=(
            jax.ShapeDtypeStruct(queries.shape, BF16),
            jax.ShapeDtypeStruct((1,), F32),
        ),
        in_specs=[pl.BlockSpec(memory_space=pltpu.HBM)] * 9,
        out_specs=(vmem, smem),
        scratch_shapes=[
            pltpu.SMEM((1,), jnp.int32),
            pltpu.SMEM((1,), F32),
            pltpu.SMEM((1,), jnp.int32),
            pltpu.VMEM(queries.shape, BF16),
            pltpu.VMEM(new_keys.shape, BF16),
            pltpu.VMEM(new_values.shape, BF16),
            pltpu.VMEM(reward_weight.shape, BF16),
            pltpu.VMEM((context, kv_width), BF16),
            pltpu.VMEM((context, kv_width), BF16),
            pltpu.VMEM((total_rows, HD), F32),
            pltpu.VMEM((total_rows, HD), F32),
            pltpu.VMEM((n, 8, HD), jnp.int32),
            pltpu.VMEM((n, total_rows, HD), BF16),
            pltpu.VMEM((n, total_rows, HD), BF16),
            pltpu.VMEM((n, 8, total_rows), F32),
            pltpu.VMEM((n, total_rows, HD), BF16),
            pltpu.VMEM((n, 8, total_rows), F32),
            pltpu.VMEM((2, 2 * steps, HD), F32),
            pltpu.SemaphoreType.DMA((7,)),
            pltpu.SemaphoreType.DMA((2,)),
            pltpu.SemaphoreType.DMA((2, n)),
            pltpu.SemaphoreType.DMA((2, n)),
            pltpu.SemaphoreType.DMA((2, n)),
            pltpu.SemaphoreType.DMA((2, n)),
            pltpu.SemaphoreType.DMA((2,)),
        ],
        compiler_params=pltpu.CompilerParams(
            collective_id=0, has_side_effects=True, vmem_limit_bytes=63 * 1024 * 1024
        ),
    )(
        lengths,
        parent_scores,
        parents,
        queries,
        new_keys,
        new_values,
        reward_weight,
        cache_keys,
        cache_values,
    )


def solution(mesh):
    beams = P(("groups", "dp"))
    split = P(("groups", "dp"), None, "tensor")
    return jax.shard_map(
        functools.partial(per_device, mesh.shape["dp"]),
        mesh=mesh,
        in_specs=(split, split, beams, beams, beams, split, split, split, P("tensor")),
        out_specs=(split, beams),
        check_vma=False,
    )
```

```python
import functools
import math

import jax
import jax.numpy as jnp
from jax import lax
from jax.experimental import pallas as pl
from jax.experimental.pallas import tpu as pltpu
from jax.sharding import PartitionSpec as P

HD = 128
MESH = pl.DeviceIdType.MESH
F32 = jnp.float32
BF16 = jnp.bfloat16


def inner_of(n):
    inner = 1
    while n % (2 * inner) == 0 and 4 * inner * inner <= n:
        inner *= 2
    return inner


def kernel(
    n,
    lengths_in,
    parent_scores_in,
    parents_in,
    queries_in,
    new_keys_in,
    new_values_in,
    reward_weight_in,
    cache_keys,
    cache_values,
    attended,
    scores,
    lengths,
    parent_scores,
    parents,
    queries,
    new_keys,
    new_values,
    reward_weight,
    keys,
    values,
    stage,
    weight,
    ids,
    asked,
    answer,
    answer_lse,
    relay,
    picked,
    got,
    got_lse,
    part,
    small_sems,
    cache_sems,
    id_sems,
    ask_sems,
    relay_sems,
    got_sems,
    lse_sems,
    part_sems,
):
    me = lax.axis_index("dp")
    inner = inner_of(n)
    outer = n // inner
    z = me // inner
    x = lax.rem(me, inner)
    core = lax.axis_index("tensor")
    steps = queries.shape[1]
    heads = queries.shape[2] // HD
    context = cache_keys.shape[1]
    kv_heads = cache_keys.shape[2] // HD
    group = heads // kv_heads
    rows = group * steps
    total_rows = heads * steps
    scale = HD ** (-0.5)
    base2 = scale * math.log2(math.e)

    small = [
        pltpu.make_async_copy(source, target, small_sems.at[i])
        for i, (source, target) in enumerate(
            (
                (queries_in, queries),
                (parents_in, parents),
                (new_keys_in, new_keys),
                (new_values_in, new_values),
                (reward_weight_in, reward_weight),
                (lengths_in, lengths),
                (parent_scores_in, parent_scores),
            )
        )
    ]
    for copy in small:
        copy.start()
    copy_keys = pltpu.make_async_copy(cache_keys.at[0], keys, cache_sems.at[0])
    copy_values = pltpu.make_async_copy(cache_values.at[0], values, cache_sems.at[1])
    copy_keys.start()
    copy_values.start()

    barrier = pltpu.get_barrier_semaphore()

    def peer(k):
        return lax.rem(me + 1 + k, n)

    def greet(k, carry):
        pl.semaphore_signal(barrier, inc=1, device_id={"dp": peer(k)}, device_id_type=MESH)
        return carry

    lax.fori_loop(0, n - 1, greet, 0)
    pl.semaphore_signal(barrier, inc=1, device_id={"tensor": 1 - core}, device_id_type=MESH)

    small[0].wait()
    small[1].wait()
    for head in range(heads):
        stage[head * steps : (head + 1) * steps, :] = queries[
            0, :, head * HD : (head + 1) * HD
        ].astype(F32)
    query = stage[...].astype(BF16)
    asked[me] = query
    ids[me] = jnp.full((8, HD), parents[0], jnp.int32)

    pl.semaphore_wait(barrier, n)

    def ask_copy(slot, to, send):
        return pltpu.make_async_remote_copy(
            src_ref=asked.at[slot],
            dst_ref=asked.at[slot],
            send_sem=ask_sems.at[0, send],
            recv_sem=ask_sems.at[1, slot],
            device_id={"dp": to},
            device_id_type=MESH,
        )

    def id_copy(slot, to):
        return pltpu.make_async_remote_copy(
            src_ref=ids.at[slot],
            dst_ref=ids.at[slot],
            send_sem=id_sems.at[0, to],
            recv_sem=id_sems.at[1, slot],
            device_id={"dp": to},
            device_id_type=MESH,
        )

    def relay_copy(source, to, far):
        return pltpu.make_async_remote_copy(
            src_ref=answer.at[far * inner + to],
            dst_ref=relay.at[far * inner + source],
            send_sem=relay_sems.at[0, far * inner + to],
            recv_sem=relay_sems.at[1, far * inner + source],
            device_id={"dp": z * inner + to},
            device_id_type=MESH,
        )

    def got_copy(source, to):
        return pltpu.make_async_remote_copy(
            src_ref=picked.at[to],
            dst_ref=got.at[source],
            send_sem=got_sems.at[0, to],
            recv_sem=got_sems.at[1, source],
            device_id={"dp": to * inner + x},
            device_id_type=MESH,
        )

    def lse_copy(slot, to):
        return pltpu.make_async_remote_copy(
            src_ref=answer_lse.at[to],
            dst_ref=got_lse.at[slot],
            send_sem=lse_sems.at[0, to],
            recv_sem=lse_sems.at[1, slot],
            device_id={"dp": to},
            device_id_type=MESH,
        )

    def far(k):
        return lax.rem(z + 1 + k, outer)

    def near(k):
        return lax.rem(x + 1 + k, inner)

    def ask_far(k, carry):
        ask_copy(me, far(k) * inner + x, far(k) * inner + x).start()
        return carry

    def ask_near(line, start):
        def body(k, carry):
            copy = ask_copy(line * inner + x, z * inner + near(k), line * inner + near(k))
            if start:
                copy.start()
            else:
                copy.wait_send()
            return carry

        lax.fori_loop(0, inner - 1, body, 0)

    def tell(k, carry):
        id_copy(me, peer(k)).start()
        return carry

    lax.fori_loop(0, outer - 1, ask_far, 0)
    ask_near(z, True)
    lax.fori_loop(0, n - 1, tell, 0)

    for copy in small[2:]:
        copy.wait()
    for head in range(heads):
        weight[head * steps : (head + 1) * steps, :] = jnp.broadcast_to(
            reward_weight[head * HD : (head + 1) * HD].astype(F32)[None], (steps, HD)
        )

    def pass_on(k, carry):
        line = lax.rem(z + outer - 1 - k, outer)
        ask_copy(line * inner + x, me, me).wait_recv()
        ask_near(line, True)
        return carry

    lax.fori_loop(0, outer - 1, pass_on, 0)

    own_keys = new_keys[0]
    own_values = new_values[0]
    row_step = lax.rem(lax.broadcasted_iota(jnp.int32, (rows, steps), 0), steps)
    causal = lax.broadcasted_iota(jnp.int32, (rows, steps), 1) <= row_step
    own_sums, own_tops, own_totals = [], [], []
    for head in range(kv_heads):
        q = query[head * rows : (head + 1) * rows]
        logits = lax.dot_general(
            q,
            own_keys[:, head * HD : (head + 1) * HD],
            (((1,), (1,)), ((), ())),
            preferred_element_type=F32,
        )
        logits = jnp.where(causal, logits * scale, -1e30)
        top = jnp.max(logits, axis=1, keepdims=True)
        weights = jnp.exp(logits - top)
        own_tops.append(top)
        own_totals.append(jnp.sum(weights, axis=1, keepdims=True))
        own_sums.append(
            jnp.dot(
                weights.astype(BF16),
                own_values[:, head * HD : (head + 1) * HD],
                preferred_element_type=F32,
            )
        )
    top_own = jnp.concatenate(own_tops, axis=0)
    total_own = jnp.concatenate(own_totals, axis=0)
    sum_own = jnp.concatenate(own_sums, axis=0)

    copy_keys.wait()
    copy_values.wait()

    def asked_wait(k, carry):
        id_copy(peer(k), me).wait_recv()
        return carry

    def passed_wait(k, carry):
        slot = lax.rem(k, outer) * inner + near(k // outer)
        ask_copy(slot, me, me).wait_recv()
        return carry

    lax.fori_loop(0, n - 1, asked_wait, 0)
    lax.fori_loop(0, outer * (inner - 1), passed_wait, 0)

    def find(slot, carry):
        first, last = carry
        mine = ids[slot] == me
        return (
            jnp.minimum(first, jnp.where(mine, slot, n)),
            jnp.maximum(last, jnp.where(mine, slot, -1)),
        )

    first, last = lax.fori_loop(
        0, n, find, (jnp.full((8, HD), n, jnp.int32), jnp.full((8, HD), -1, jnp.int32))
    )
    first = jnp.minimum(jnp.max(first), n - 1)
    last = jnp.maximum(jnp.max(last), 0)
    both = (asked[first], asked[last])

    place = lax.broadcasted_iota(jnp.int32, (1, context), 1)
    bias = jnp.where(place < lengths[0], 0.0, -1e30)
    outs, lses = ([], []), ([], [])
    for head in range(kv_heads):
        q = jnp.concatenate([b[head * rows : (head + 1) * rows] for b in both], axis=0)
        logits = lax.dot_general(
            q,
            keys[:, head * HD : (head + 1) * HD],
            (((1,), (1,)), ((), ())),
            preferred_element_type=F32,
        )
        logits = logits + bias
        top = jnp.max(logits, axis=1, keepdims=True)
        weights = jnp.exp2((logits - top) * base2)
        total = jnp.sum(weights, axis=1, keepdims=True)
        summed = jnp.dot(
            weights.astype(BF16),
            values[:, head * HD : (head + 1) * HD],
            preferred_element_type=F32,
        )
        out = (summed / total).astype(BF16)
        lse = top * scale + jnp.log(total)
        for child in range(2):
            outs[child].append(out[child * rows : (child + 1) * rows])
            lses[child].append(lse[child * rows : (child + 1) * rows])

    eye = lax.broadcasted_iota(jnp.int32, (total_rows, total_rows), 0) == lax.broadcasted_iota(
        jnp.int32, (total_rows, total_rows), 1
    )
    out_by_child = [jnp.concatenate(o, axis=0) for o in outs]
    lse_by_child = [
        jnp.sum(jnp.where(eye, jnp.concatenate(l, axis=0), 0.0), axis=0, keepdims=True)
        for l in lses
    ]
    score_row = jnp.full((1, total_rows), parent_scores[0], F32)

    def pick(slot):
        return jnp.where(slot == first, out_by_child[0], out_by_child[1])

    def reply_near(k, carry):
        line = lax.rem(z + 1 + lax.rem(k, outer), outer)
        to = near(k // outer)
        answer[line * inner + to] = pick(line * inner + to)
        relay_copy(x, to, line).start()
        return carry

    lax.fori_loop(0, outer * (inner - 1), reply_near, 0)

    def reply_lse(k, carry):
        to = peer(k)
        answer_lse[to, 0:1, :] = jnp.where(to == first, lse_by_child[0], lse_by_child[1])
        answer_lse[to, 1:2, :] = score_row
        lse_copy(me, to).start()
        return carry

    lax.fori_loop(0, n - 1, reply_lse, 0)
    got_lse[me, 0:1, :] = jnp.where(me == first, lse_by_child[0], lse_by_child[1])
    got_lse[me, 1:2, :] = score_row

    def collect(line):
        slot = line * inner + x
        parent = jnp.max(ids[slot])
        row = pick(slot)
        for k in range(inner - 1):
            relay_copy(near(k), x, line).wait_recv()
            row = jnp.where(
                parent == z * inner + near(k), relay[line * inner + near(k)], row
            )
        return row

    def reply_far(k, carry):
        to = far(k)
        picked[to] = collect(to)
        got_copy(z, to).start()
        return carry

    lax.fori_loop(0, outer - 1, reply_far, 0)
    got[z] = collect(z)

    def lse_wait(k, carry):
        lse_copy(peer(k), me).wait_recv()
        return carry

    lax.fori_loop(0, n - 1, lse_wait, 0)

    def reply_wait(k, carry):
        got_copy(far(k), z).wait_recv()
        return carry

    lax.fori_loop(0, outer - 1, reply_wait, 0)

    holder = parents[0]
    parent_out = got[holder // inner].astype(F32)
    lse_rows = got_lse[holder]
    inherited = jnp.max(lse_rows[1:2, :])
    parent_lse = jnp.sum(jnp.where(eye, lse_rows[0:1, :], 0.0), axis=1, keepdims=True)
    top = jnp.maximum(parent_lse, top_own)
    factor_parent = jnp.exp(parent_lse - top)
    factor_own = jnp.exp(top_own - top)
    merged = (parent_out * factor_parent + sum_own * factor_own) / (
        factor_parent + total_own * factor_own
    )
    output = merged.astype(BF16).astype(F32)
    stage[...] = output
    product = output * weight[...]
    tall = 2 * steps
    partial = product[0:tall]
    for i in range(1, total_rows // tall):
        partial = partial + product[i * tall : (i + 1) * tall]
    part[0] = partial
    part_copy = pltpu.make_async_remote_copy(
        src_ref=part.at[0],
        dst_ref=part.at[1],
        send_sem=part_sems.at[0],
        recv_sem=part_sems.at[1],
        device_id={"tensor": 1 - core},
        device_id_type=MESH,
    )
    part_copy.start()
    for head in range(heads):
        attended[0, :, head * HD : (head + 1) * HD] = stage[
            head * steps : (head + 1) * steps, :
        ].astype(BF16)

    def sent_wait(k, carry):
        id_copy(me, peer(k)).wait_send()
        lse_copy(me, peer(k)).wait_send()
        return carry

    def far_wait(k, carry):
        ask_copy(me, far(k) * inner + x, far(k) * inner + x).wait_send()
        got_copy(z, far(k)).wait_send()
        return carry

    def near_wait(k, carry):
        ask_near(k, False)
        return carry

    def relay_wait(k, carry):
        relay_copy(x, near(k // outer), lax.rem(k, outer)).wait_send()
        return carry

    lax.fori_loop(0, n - 1, sent_wait, 0)
    lax.fori_loop(0, outer - 1, far_wait, 0)
    lax.fori_loop(0, outer, near_wait, 0)
    lax.fori_loop(0, outer * (inner - 1), relay_wait, 0)
    part_copy.wait()
    reward = jnp.sum(part[0] + part[1], axis=1, keepdims=True)
    reward = reward[0:steps] + reward[steps : 2 * steps]
    logs = jnp.minimum(reward, 0.0) - jnp.log1p(jnp.exp(-jnp.abs(reward)))
    scores[0] = inherited + jnp.sum(logs)


def per_device(
    n,
    cache_keys,
    cache_values,
    lengths,
    parent_scores,
    parents,
    queries,
    new_keys,
    new_values,
    reward_weight,
):
    steps = queries.shape[1]
    width = queries.shape[2]
    context, kv_width = cache_keys.shape[1:]
    total_rows = steps * width // HD
    vmem = pl.BlockSpec(memory_space=pltpu.VMEM)
    smem = pl.BlockSpec(memory_space=pltpu.SMEM)
    return pl.pallas_call(
        functools.partial(kernel, n),
        out_shape=(
            jax.ShapeDtypeStruct(queries.shape, BF16),
            jax.ShapeDtypeStruct((1,), F32),
        ),
        in_specs=[pl.BlockSpec(memory_space=pltpu.HBM)] * 9,
        out_specs=(vmem, smem),
        scratch_shapes=[
            pltpu.SMEM((1,), jnp.int32),
            pltpu.SMEM((1,), F32),
            pltpu.SMEM((1,), jnp.int32),
            pltpu.VMEM(queries.shape, BF16),
            pltpu.VMEM(new_keys.shape, BF16),
            pltpu.VMEM(new_values.shape, BF16),
            pltpu.VMEM(reward_weight.shape, BF16),
            pltpu.VMEM((context, kv_width), BF16),
            pltpu.VMEM((context, kv_width), BF16),
            pltpu.VMEM((total_rows, HD), F32),
            pltpu.VMEM((total_rows, HD), F32),
            pltpu.VMEM((n, 8, HD), jnp.int32),
            pltpu.VMEM((n, total_rows, HD), BF16),
            pltpu.VMEM((n, total_rows, HD), BF16),
            pltpu.VMEM((n, 8, total_rows), F32),
            pltpu.VMEM((n, total_rows, HD), BF16),
            pltpu.VMEM((n // inner_of(n), total_rows, HD), BF16),
            pltpu.VMEM((n // inner_of(n), total_rows, HD), BF16),
            pltpu.VMEM((n, 8, total_rows), F32),
            pltpu.VMEM((2, 2 * steps, HD), F32),
            pltpu.SemaphoreType.DMA((7,)),
            pltpu.SemaphoreType.DMA((2,)),
            pltpu.SemaphoreType.DMA((2, n)),
            pltpu.SemaphoreType.DMA((2, n)),
            pltpu.SemaphoreType.DMA((2, n)),
            pltpu.SemaphoreType.DMA((2, n)),
            pltpu.SemaphoreType.DMA((2, n)),
            pltpu.SemaphoreType.DMA((2,)),
        ],
        compiler_params=pltpu.CompilerParams(
            collective_id=0, has_side_effects=True, vmem_limit_bytes=63 * 1024 * 1024
        ),
    )(
        lengths,
        parent_scores,
        parents,
        queries,
        new_keys,
        new_values,
        reward_weight,
        cache_keys,
        cache_values,
    )


def solution(mesh):
    beams = P(("groups", "dp"))
    split = P(("groups", "dp"), None, "tensor")
    return jax.shard_map(
        functools.partial(per_device, mesh.shape["dp"]),
        mesh=mesh,
        in_specs=(split, split, beams, beams, beams, split, split, split, P("tensor")),
        out_specs=(split, beams),
        check_vma=False,
    )
```

```python
import functools
import math

import jax
import jax.numpy as jnp
from jax import lax
from jax.experimental import pallas as pl
from jax.experimental.pallas import tpu as pltpu
from jax.sharding import PartitionSpec as P

HD = 128
MESH = pl.DeviceIdType.MESH
F32 = jnp.float32
BF16 = jnp.bfloat16


def inner_of(n):
    inner = 1
    while n % (2 * inner) == 0 and 4 * inner * inner <= n:
        inner *= 2
    return inner


def kernel(
    n,
    lengths_in,
    parent_scores_in,
    parents_in,
    queries_in,
    new_keys_in,
    new_values_in,
    reward_weight_in,
    cache_keys,
    cache_values,
    attended,
    scores,
    lengths,
    parent_scores,
    parents,
    queries,
    new_keys,
    new_values,
    reward_weight,
    keys,
    values,
    stage,
    weight,
    ids,
    asked,
    answer,
    answer_lse,
    got,
    got_lse,
    part,
    small_sems,
    cache_sems,
    id_sems,
    ask_sems,
    got_sems,
    lse_sems,
    part_sems,
):
    me = lax.axis_index("dp")
    inner = inner_of(n)
    outer = n // inner
    z = me // inner
    x = lax.rem(me, inner)
    core = lax.axis_index("tensor")
    steps = queries.shape[1]
    heads = queries.shape[2] // HD
    context = cache_keys.shape[1]
    kv_heads = cache_keys.shape[2] // HD
    group = heads // kv_heads
    rows = group * steps
    total_rows = heads * steps
    scale = HD ** (-0.5)
    base2 = scale * math.log2(math.e)

    small = [
        pltpu.make_async_copy(source, target, small_sems.at[i])
        for i, (source, target) in enumerate(
            (
                (queries_in, queries),
                (parents_in, parents),
                (new_keys_in, new_keys),
                (new_values_in, new_values),
                (reward_weight_in, reward_weight),
                (lengths_in, lengths),
                (parent_scores_in, parent_scores),
            )
        )
    ]
    for copy in small:
        copy.start()
    copy_keys = pltpu.make_async_copy(cache_keys.at[0], keys, cache_sems.at[0])
    copy_values = pltpu.make_async_copy(cache_values.at[0], values, cache_sems.at[1])
    copy_keys.start()
    copy_values.start()

    barrier = pltpu.get_barrier_semaphore()

    def peer(k):
        return lax.rem(me + 1 + k, n)

    def greet(k, carry):
        pl.semaphore_signal(barrier, inc=1, device_id={"dp": peer(k)}, device_id_type=MESH)
        return carry

    lax.fori_loop(0, n - 1, greet, 0)
    pl.semaphore_signal(barrier, inc=1, device_id={"tensor": 1 - core}, device_id_type=MESH)

    small[0].wait()
    small[1].wait()
    for head in range(heads):
        stage[head * steps : (head + 1) * steps, :] = queries[
            0, :, head * HD : (head + 1) * HD
        ].astype(F32)
    query = stage[...].astype(BF16)
    asked[me] = query
    ids[me] = jnp.full((8, HD), parents[0], jnp.int32)

    pl.semaphore_wait(barrier, n)

    def ask_copy(slot, to, send):
        return pltpu.make_async_remote_copy(
            src_ref=asked.at[slot],
            dst_ref=asked.at[slot],
            send_sem=ask_sems.at[0, send],
            recv_sem=ask_sems.at[1, slot],
            device_id={"dp": to},
            device_id_type=MESH,
        )

    def id_copy(slot, to):
        return pltpu.make_async_remote_copy(
            src_ref=ids.at[slot],
            dst_ref=ids.at[slot],
            send_sem=id_sems.at[0, to],
            recv_sem=id_sems.at[1, slot],
            device_id={"dp": to},
            device_id_type=MESH,
        )

    def got_copy(slot, to):
        return pltpu.make_async_remote_copy(
            src_ref=answer.at[to],
            dst_ref=got.at[slot],
            send_sem=got_sems.at[0, to],
            recv_sem=got_sems.at[1, slot],
            device_id={"dp": to},
            device_id_type=MESH,
        )

    def lse_copy(slot, to):
        return pltpu.make_async_remote_copy(
            src_ref=answer_lse.at[to],
            dst_ref=got_lse.at[slot],
            send_sem=lse_sems.at[0, to],
            recv_sem=lse_sems.at[1, slot],
            device_id={"dp": to},
            device_id_type=MESH,
        )

    def far(k):
        return lax.rem(z + 1 + k, outer)

    def near(k):
        return lax.rem(x + 1 + k, inner)

    def ask_far(k, carry):
        ask_copy(me, far(k) * inner + x, far(k) * inner + x).start()
        return carry

    def ask_near(line, start):
        def body(k, carry):
            copy = ask_copy(line * inner + x, z * inner + near(k), line * inner + near(k))
            if start:
                copy.start()
            else:
                copy.wait_send()
            return carry

        lax.fori_loop(0, inner - 1, body, 0)

    def tell(k, carry):
        id_copy(me, peer(k)).start()
        return carry

    lax.fori_loop(0, outer - 1, ask_far, 0)
    ask_near(z, True)
    lax.fori_loop(0, n - 1, tell, 0)

    for copy in small[2:]:
        copy.wait()
    for head in range(heads):
        weight[head * steps : (head + 1) * steps, :] = jnp.broadcast_to(
            reward_weight[head * HD : (head + 1) * HD].astype(F32)[None], (steps, HD)
        )

    def pass_on(k, carry):
        line = lax.rem(z + outer - 1 - k, outer)
        ask_copy(line * inner + x, me, me).wait_recv()
        ask_near(line, True)
        return carry

    lax.fori_loop(0, outer - 1, pass_on, 0)

    own_keys = new_keys[0]
    own_values = new_values[0]
    row_step = lax.rem(lax.broadcasted_iota(jnp.int32, (rows, steps), 0), steps)
    causal = lax.broadcasted_iota(jnp.int32, (rows, steps), 1) <= row_step
    own_sums, own_tops, own_totals = [], [], []
    for head in range(kv_heads):
        q = query[head * rows : (head + 1) * rows]
        logits = lax.dot_general(
            q,
            own_keys[:, head * HD : (head + 1) * HD],
            (((1,), (1,)), ((), ())),
            preferred_element_type=F32,
        )
        logits = jnp.where(causal, logits * scale, -1e30)
        top = jnp.max(logits, axis=1, keepdims=True)
        weights = jnp.exp(logits - top)
        own_tops.append(top)
        own_totals.append(jnp.sum(weights, axis=1, keepdims=True))
        own_sums.append(
            jnp.dot(
                weights.astype(BF16),
                own_values[:, head * HD : (head + 1) * HD],
                preferred_element_type=F32,
            )
        )
    top_own = jnp.concatenate(own_tops, axis=0)
    total_own = jnp.concatenate(own_totals, axis=0)
    sum_own = jnp.concatenate(own_sums, axis=0)

    copy_keys.wait()
    copy_values.wait()

    def asked_wait(k, carry):
        id_copy(peer(k), me).wait_recv()
        return carry

    def passed_wait(k, carry):
        slot = lax.rem(k, outer) * inner + near(k // outer)
        ask_copy(slot, me, me).wait_recv()
        return carry

    lax.fori_loop(0, n - 1, asked_wait, 0)
    lax.fori_loop(0, outer * (inner - 1), passed_wait, 0)

    def find(slot, carry):
        first, last = carry
        mine = ids[slot] == me
        return (
            jnp.minimum(first, jnp.where(mine, slot, n)),
            jnp.maximum(last, jnp.where(mine, slot, -1)),
        )

    first, last = lax.fori_loop(
        0, n, find, (jnp.full((8, HD), n, jnp.int32), jnp.full((8, HD), -1, jnp.int32))
    )
    first = jnp.minimum(jnp.max(first), n - 1)
    last = jnp.maximum(jnp.max(last), 0)
    both = (asked[first], asked[last])

    place = lax.broadcasted_iota(jnp.int32, (1, context), 1)
    bias = jnp.where(place < lengths[0], 0.0, -1e30)
    outs, lses = ([], []), ([], [])
    for head in range(kv_heads):
        q = jnp.concatenate([b[head * rows : (head + 1) * rows] for b in both], axis=0)
        logits = lax.dot_general(
            q,
            keys[:, head * HD : (head + 1) * HD],
            (((1,), (1,)), ((), ())),
            preferred_element_type=F32,
        )
        logits = logits + bias
        top = jnp.max(logits, axis=1, keepdims=True)
        weights = jnp.exp2((logits - top) * base2)
        total = jnp.sum(weights, axis=1, keepdims=True)
        summed = jnp.dot(
            weights.astype(BF16),
            values[:, head * HD : (head + 1) * HD],
            preferred_element_type=F32,
        )
        out = (summed / total).astype(BF16)
        lse = top * scale + jnp.log(total)
        for child in range(2):
            outs[child].append(out[child * rows : (child + 1) * rows])
            lses[child].append(lse[child * rows : (child + 1) * rows])

    eye = lax.broadcasted_iota(jnp.int32, (total_rows, total_rows), 0) == lax.broadcasted_iota(
        jnp.int32, (total_rows, total_rows), 1
    )
    out_by_child = [jnp.concatenate(o, axis=0) for o in outs]
    lse_by_child = [
        jnp.sum(jnp.where(eye, jnp.concatenate(l, axis=0), 0.0), axis=0, keepdims=True)
        for l in lses
    ]
    score_row = jnp.full((1, total_rows), parent_scores[0], F32)

    def reply(k, carry):
        to = peer(k)
        answer[to] = jnp.where(to == first, out_by_child[0], out_by_child[1])
        answer_lse[to, 0:1, :] = jnp.where(to == first, lse_by_child[0], lse_by_child[1])
        answer_lse[to, 1:2, :] = score_row
        got_copy(me, to).start()
        lse_copy(me, to).start()
        return carry

    lax.fori_loop(0, n - 1, reply, 0)
    got[me] = jnp.where(me == first, out_by_child[0], out_by_child[1])
    got_lse[me, 0:1, :] = jnp.where(me == first, lse_by_child[0], lse_by_child[1])
    got_lse[me, 1:2, :] = score_row

    def reply_wait(k, carry):
        got_copy(peer(k), me).wait_recv()
        lse_copy(peer(k), me).wait_recv()
        return carry

    lax.fori_loop(0, n - 1, reply_wait, 0)

    holder = parents[0]
    parent_out = got[holder].astype(F32)
    lse_rows = got_lse[holder]
    inherited = jnp.max(lse_rows[1:2, :])
    parent_lse = jnp.sum(jnp.where(eye, lse_rows[0:1, :], 0.0), axis=1, keepdims=True)
    top = jnp.maximum(parent_lse, top_own)
    factor_parent = jnp.exp(parent_lse - top)
    factor_own = jnp.exp(top_own - top)
    merged = (parent_out * factor_parent + sum_own * factor_own) / (
        factor_parent + total_own * factor_own
    )
    output = merged.astype(BF16).astype(F32)
    stage[...] = output
    product = output * weight[...]
    tall = 2 * steps
    partial = product[0:tall]
    for i in range(1, total_rows // tall):
        partial = partial + product[i * tall : (i + 1) * tall]
    part[0] = partial
    part_copy = pltpu.make_async_remote_copy(
        src_ref=part.at[0],
        dst_ref=part.at[1],
        send_sem=part_sems.at[0],
        recv_sem=part_sems.at[1],
        device_id={"tensor": 1 - core},
        device_id_type=MESH,
    )
    part_copy.start()
    for head in range(heads):
        attended[0, :, head * HD : (head + 1) * HD] = stage[
            head * steps : (head + 1) * steps, :
        ].astype(BF16)

    def sent_wait(k, carry):
        id_copy(me, peer(k)).wait_send()
        lse_copy(me, peer(k)).wait_send()
        got_copy(me, peer(k)).wait_send()
        return carry

    def far_wait(k, carry):
        ask_copy(me, far(k) * inner + x, far(k) * inner + x).wait_send()
        return carry

    def near_wait(k, carry):
        ask_near(k, False)
        return carry

    lax.fori_loop(0, n - 1, sent_wait, 0)
    lax.fori_loop(0, outer - 1, far_wait, 0)
    lax.fori_loop(0, outer, near_wait, 0)
    part_copy.wait()
    reward = jnp.sum(part[0] + part[1], axis=1, keepdims=True)
    reward = reward[0:steps] + reward[steps : 2 * steps]
    logs = jnp.minimum(reward, 0.0) - jnp.log1p(jnp.exp(-jnp.abs(reward)))
    scores[0] = inherited + jnp.sum(logs)


def per_device(
    n,
    cache_keys,
    cache_values,
    lengths,
    parent_scores,
    parents,
    queries,
    new_keys,
    new_values,
    reward_weight,
):
    steps = queries.shape[1]
    width = queries.shape[2]
    context, kv_width = cache_keys.shape[1:]
    total_rows = steps * width // HD
    vmem = pl.BlockSpec(memory_space=pltpu.VMEM)
    smem = pl.BlockSpec(memory_space=pltpu.SMEM)
    return pl.pallas_call(
        functools.partial(kernel, n),
        out_shape=(
            jax.ShapeDtypeStruct(queries.shape, BF16),
            jax.ShapeDtypeStruct((1,), F32),
        ),
        in_specs=[pl.BlockSpec(memory_space=pltpu.HBM)] * 9,
        out_specs=(vmem, smem),
        scratch_shapes=[
            pltpu.SMEM((1,), jnp.int32),
            pltpu.SMEM((1,), F32),
            pltpu.SMEM((1,), jnp.int32),
            pltpu.VMEM(queries.shape, BF16),
            pltpu.VMEM(new_keys.shape, BF16),
            pltpu.VMEM(new_values.shape, BF16),
            pltpu.VMEM(reward_weight.shape, BF16),
            pltpu.VMEM((context, kv_width), BF16),
            pltpu.VMEM((context, kv_width), BF16),
            pltpu.VMEM((total_rows, HD), F32),
            pltpu.VMEM((total_rows, HD), F32),
            pltpu.VMEM((n, 8, HD), jnp.int32),
            pltpu.VMEM((n, total_rows, HD), BF16),
            pltpu.VMEM((n, total_rows, HD), BF16),
            pltpu.VMEM((n, 8, total_rows), F32),
            pltpu.VMEM((n, total_rows, HD), BF16),
            pltpu.VMEM((n, 8, total_rows), F32),
            pltpu.VMEM((2, 2 * steps, HD), F32),
            pltpu.SemaphoreType.DMA((7,)),
            pltpu.SemaphoreType.DMA((2,)),
            pltpu.SemaphoreType.DMA((2, n)),
            pltpu.SemaphoreType.DMA((2, n)),
            pltpu.SemaphoreType.DMA((2, n)),
            pltpu.SemaphoreType.DMA((2, n)),
            pltpu.SemaphoreType.DMA((2,)),
        ],
        compiler_params=pltpu.CompilerParams(
            collective_id=0, has_side_effects=True, vmem_limit_bytes=63 * 1024 * 1024
        ),
    )(
        lengths,
        parent_scores,
        parents,
        queries,
        new_keys,
        new_values,
        reward_weight,
        cache_keys,
        cache_values,
    )


def solution(mesh):
    beams = P(("groups", "dp"))
    split = P(("groups", "dp"), None, "tensor")
    return jax.shard_map(
        functools.partial(per_device, mesh.shape["dp"]),
        mesh=mesh,
        in_specs=(split, split, beams, beams, beams, split, split, split, P("tensor")),
        out_specs=(split, beams),
        check_vma=False,
    )
```

```python
import functools
import math

import jax
import jax.numpy as jnp
from jax import lax
from jax.experimental import pallas as pl
from jax.experimental.pallas import tpu as pltpu
from jax.sharding import PartitionSpec as P

HD = 128
MESH = pl.DeviceIdType.MESH
F32 = jnp.float32
BF16 = jnp.bfloat16


def inner_of(n):
    inner = 1
    while n % (2 * inner) == 0 and 4 * inner * inner <= n:
        inner *= 2
    return inner


def each_peer(n, body):
    if n <= 16:
        for k in range(n - 1):
            body(k, 0)
    else:
        lax.fori_loop(0, n - 1, body, 0)


def kernel(
    n,
    lengths_in,
    parent_scores_in,
    parents_in,
    queries_in,
    new_keys_in,
    new_values_in,
    reward_weight_in,
    cache_keys,
    cache_values,
    attended,
    scores,
    lengths,
    parent_scores,
    parents,
    queries,
    new_keys,
    new_values,
    reward_weight,
    keys,
    values,
    stage,
    weight,
    ids,
    asked,
    answer,
    answer_lse,
    got,
    got_lse,
    part,
    small_sems,
    cache_sems,
    id_sems,
    ask_sems,
    got_sems,
    lse_sems,
    part_sems,
):
    me = lax.axis_index("dp")
    inner = inner_of(n)
    outer = n // inner
    z = me // inner
    x = lax.rem(me, inner)
    core = lax.axis_index("tensor")
    steps = queries.shape[1]
    heads = queries.shape[2] // HD
    context = cache_keys.shape[1]
    kv_heads = cache_keys.shape[2] // HD
    group = heads // kv_heads
    rows = group * steps
    total_rows = heads * steps
    scale = HD ** (-0.5)
    base2 = scale * math.log2(math.e)

    small = [
        pltpu.make_async_copy(source, target, small_sems.at[i])
        for i, (source, target) in enumerate(
            (
                (queries_in, queries),
                (parents_in, parents),
                (new_keys_in, new_keys),
                (new_values_in, new_values),
                (reward_weight_in, reward_weight),
                (lengths_in, lengths),
                (parent_scores_in, parent_scores),
            )
        )
    ]
    for copy in small:
        copy.start()
    copy_keys = pltpu.make_async_copy(cache_keys.at[0], keys, cache_sems.at[0])
    copy_values = pltpu.make_async_copy(cache_values.at[0], values, cache_sems.at[1])
    copy_keys.start()
    copy_values.start()

    barrier = pltpu.get_barrier_semaphore()

    def peer(k):
        return jnp.where(me + 1 + k >= n, me + 1 + k - n, me + 1 + k)

    def greet(k, carry):
        pl.semaphore_signal(barrier, inc=1, device_id={"dp": peer(k)}, device_id_type=MESH)
        return carry

    each_peer(n, greet)
    pl.semaphore_signal(barrier, inc=1, device_id={"tensor": 1 - core}, device_id_type=MESH)

    small[0].wait()
    small[1].wait()
    for head in range(heads):
        stage[head * steps : (head + 1) * steps, :] = queries[
            0, :, head * HD : (head + 1) * HD
        ].astype(F32)
    query = stage[...].astype(BF16)
    asked[me] = query
    ids[me] = jnp.full((8, HD), parents[0], jnp.int32)

    pl.semaphore_wait(barrier, n)

    def ask_copy(slot, to, send):
        return pltpu.make_async_remote_copy(
            src_ref=asked.at[slot],
            dst_ref=asked.at[slot],
            send_sem=ask_sems.at[0, send],
            recv_sem=ask_sems.at[1, slot],
            device_id={"dp": to},
            device_id_type=MESH,
        )

    def id_copy(slot, to):
        return pltpu.make_async_remote_copy(
            src_ref=ids.at[slot],
            dst_ref=ids.at[slot],
            send_sem=id_sems.at[0, to],
            recv_sem=id_sems.at[1, slot],
            device_id={"dp": to},
            device_id_type=MESH,
        )

    def got_copy(slot, to):
        return pltpu.make_async_remote_copy(
            src_ref=answer.at[to],
            dst_ref=got.at[slot],
            send_sem=got_sems.at[0, to],
            recv_sem=got_sems.at[1, slot],
            device_id={"dp": to},
            device_id_type=MESH,
        )

    def lse_copy(slot, to):
        return pltpu.make_async_remote_copy(
            src_ref=answer_lse.at[to],
            dst_ref=got_lse.at[slot],
            send_sem=lse_sems.at[0, to],
            recv_sem=lse_sems.at[1, slot],
            device_id={"dp": to},
            device_id_type=MESH,
        )

    def far(k):
        return lax.rem(z + 1 + k, outer)

    def near(k):
        return lax.rem(x + 1 + k, inner)

    def ask_far(k, carry):
        ask_copy(me, far(k) * inner + x, far(k) * inner + x).start()
        return carry

    def ask_near(line, start):
        def body(k, carry):
            copy = ask_copy(line * inner + x, z * inner + near(k), line * inner + near(k))
            if start:
                copy.start()
            else:
                copy.wait_send()
            return carry

        lax.fori_loop(0, inner - 1, body, 0)

    def tell(k, carry):
        id_copy(me, peer(k)).start()
        return carry

    lax.fori_loop(0, outer - 1, ask_far, 0)
    ask_near(z, True)
    each_peer(n, tell)

    for copy in small[2:]:
        copy.wait()
    for head in range(heads):
        weight[head * steps : (head + 1) * steps, :] = jnp.broadcast_to(
            reward_weight[head * HD : (head + 1) * HD].astype(F32)[None], (steps, HD)
        )

    def pass_on(k, carry):
        line = lax.rem(z + outer - 1 - k, outer)
        ask_copy(line * inner + x, me, me).wait_recv()
        ask_near(line, True)
        return carry

    lax.fori_loop(0, outer - 1, pass_on, 0)

    own_keys = new_keys[0]
    own_values = new_values[0]
    row_step = lax.rem(lax.broadcasted_iota(jnp.int32, (rows, steps), 0), steps)
    causal = lax.broadcasted_iota(jnp.int32, (rows, steps), 1) <= row_step
    own_sums, own_tops, own_totals = [], [], []
    for head in range(kv_heads):
        q = query[head * rows : (head + 1) * rows]
        logits = lax.dot_general(
            q,
            own_keys[:, head * HD : (head + 1) * HD],
            (((1,), (1,)), ((), ())),
            preferred_element_type=F32,
        )
        logits = jnp.where(causal, logits * scale, -1e30)
        top = jnp.max(logits, axis=1, keepdims=True)
        weights = jnp.exp(logits - top)
        own_tops.append(top)
        own_totals.append(jnp.sum(weights, axis=1, keepdims=True))
        own_sums.append(
            jnp.dot(
                weights.astype(BF16),
                own_values[:, head * HD : (head + 1) * HD],
                preferred_element_type=F32,
            )
        )
    top_own = jnp.concatenate(own_tops, axis=0)
    total_own = jnp.concatenate(own_totals, axis=0)
    sum_own = jnp.concatenate(own_sums, axis=0)

    copy_keys.wait()
    copy_values.wait()

    def asked_wait(k, carry):
        id_copy(peer(k), me).wait_recv()
        return carry

    def passed_wait(k, carry):
        slot = lax.rem(k, outer) * inner + near(k // outer)
        ask_copy(slot, me, me).wait_recv()
        return carry

    each_peer(n, asked_wait)
    lax.fori_loop(0, outer * (inner - 1), passed_wait, 0)

    def find(slot, carry):
        first, last = carry
        mine = ids[slot] == me
        return (
            jnp.minimum(first, jnp.where(mine, slot, n)),
            jnp.maximum(last, jnp.where(mine, slot, -1)),
        )

    first, last = lax.fori_loop(
        0,
        n,
        find,
        (jnp.full((8, HD), n, jnp.int32), jnp.full((8, HD), -1, jnp.int32)),
        unroll=n <= 16,
    )
    first = jnp.minimum(jnp.max(first), n - 1)
    last = jnp.maximum(jnp.max(last), 0)
    both = (asked[first], asked[last])

    place = lax.broadcasted_iota(jnp.int32, (1, context), 1)
    bias = jnp.where(place < lengths[0], 0.0, -1e30)
    outs, lses = ([], []), ([], [])
    for head in range(kv_heads):
        q = jnp.concatenate([b[head * rows : (head + 1) * rows] for b in both], axis=0)
        logits = lax.dot_general(
            q,
            keys[:, head * HD : (head + 1) * HD],
            (((1,), (1,)), ((), ())),
            preferred_element_type=F32,
        )
        logits = logits + bias
        top = jnp.max(logits, axis=1, keepdims=True)
        weights = jnp.exp2((logits - top) * base2)
        total = jnp.sum(weights, axis=1, keepdims=True)
        summed = jnp.dot(
            weights.astype(BF16),
            values[:, head * HD : (head + 1) * HD],
            preferred_element_type=F32,
        )
        out = (summed / total).astype(BF16)
        lse = top * scale + jnp.log(total)
        for child in range(2):
            outs[child].append(out[child * rows : (child + 1) * rows])
            lses[child].append(lse[child * rows : (child + 1) * rows])

    eye = lax.broadcasted_iota(jnp.int32, (total_rows, total_rows), 0) == lax.broadcasted_iota(
        jnp.int32, (total_rows, total_rows), 1
    )
    out_by_child = [jnp.concatenate(o, axis=0) for o in outs]
    lse_by_child = [
        jnp.sum(jnp.where(eye, jnp.concatenate(l, axis=0), 0.0), axis=0, keepdims=True)
        for l in lses
    ]
    score_row = jnp.full((1, total_rows), parent_scores[0], F32)

    def reply(k, carry):
        to = peer(k)
        answer[to] = jnp.where(to == first, out_by_child[0], out_by_child[1])
        answer_lse[to, 0:1, :] = jnp.where(to == first, lse_by_child[0], lse_by_child[1])
        answer_lse[to, 1:2, :] = score_row
        got_copy(me, to).start()
        lse_copy(me, to).start()
        return carry

    each_peer(n, reply)
    got[me] = jnp.where(me == first, out_by_child[0], out_by_child[1])
    got_lse[me, 0:1, :] = jnp.where(me == first, lse_by_child[0], lse_by_child[1])
    got_lse[me, 1:2, :] = score_row

    def reply_wait(k, carry):
        got_copy(peer(k), me).wait_recv()
        lse_copy(peer(k), me).wait_recv()
        return carry

    each_peer(n, reply_wait)

    holder = parents[0]
    parent_out = got[holder].astype(F32)
    lse_rows = got_lse[holder]
    inherited = jnp.max(lse_rows[1:2, :])
    parent_lse = jnp.sum(jnp.where(eye, lse_rows[0:1, :], 0.0), axis=1, keepdims=True)
    top = jnp.maximum(parent_lse, top_own)
    factor_parent = jnp.exp(parent_lse - top)
    factor_own = jnp.exp(top_own - top)
    merged = (parent_out * factor_parent + sum_own * factor_own) / (
        factor_parent + total_own * factor_own
    )
    output = merged.astype(BF16).astype(F32)
    stage[...] = output
    product = output * weight[...]
    tall = 2 * steps
    partial = product[0:tall]
    for i in range(1, total_rows // tall):
        partial = partial + product[i * tall : (i + 1) * tall]
    part[0] = partial
    part_copy = pltpu.make_async_remote_copy(
        src_ref=part.at[0],
        dst_ref=part.at[1],
        send_sem=part_sems.at[0],
        recv_sem=part_sems.at[1],
        device_id={"tensor": 1 - core},
        device_id_type=MESH,
    )
    part_copy.start()
    for head in range(heads):
        attended[0, :, head * HD : (head + 1) * HD] = stage[
            head * steps : (head + 1) * steps, :
        ].astype(BF16)

    def sent_wait(k, carry):
        id_copy(me, peer(k)).wait_send()
        lse_copy(me, peer(k)).wait_send()
        got_copy(me, peer(k)).wait_send()
        return carry

    def far_wait(k, carry):
        ask_copy(me, far(k) * inner + x, far(k) * inner + x).wait_send()
        return carry

    def near_wait(k, carry):
        ask_near(k, False)
        return carry

    each_peer(n, sent_wait)
    lax.fori_loop(0, outer - 1, far_wait, 0)
    lax.fori_loop(0, outer, near_wait, 0)
    part_copy.wait()
    reward = jnp.sum(part[0] + part[1], axis=1, keepdims=True)
    reward = reward[0:steps] + reward[steps : 2 * steps]
    logs = jnp.minimum(reward, 0.0) - jnp.log1p(jnp.exp(-jnp.abs(reward)))
    scores[0] = inherited + jnp.sum(logs)


def per_device(
    n,
    cache_keys,
    cache_values,
    lengths,
    parent_scores,
    parents,
    queries,
    new_keys,
    new_values,
    reward_weight,
):
    steps = queries.shape[1]
    width = queries.shape[2]
    context, kv_width = cache_keys.shape[1:]
    total_rows = steps * width // HD
    vmem = pl.BlockSpec(memory_space=pltpu.VMEM)
    smem = pl.BlockSpec(memory_space=pltpu.SMEM)
    return pl.pallas_call(
        functools.partial(kernel, n),
        out_shape=(
            jax.ShapeDtypeStruct(queries.shape, BF16),
            jax.ShapeDtypeStruct((1,), F32),
        ),
        in_specs=[pl.BlockSpec(memory_space=pltpu.HBM)] * 9,
        out_specs=(vmem, smem),
        scratch_shapes=[
            pltpu.SMEM((1,), jnp.int32),
            pltpu.SMEM((1,), F32),
            pltpu.SMEM((1,), jnp.int32),
            pltpu.VMEM(queries.shape, BF16),
            pltpu.VMEM(new_keys.shape, BF16),
            pltpu.VMEM(new_values.shape, BF16),
            pltpu.VMEM(reward_weight.shape, BF16),
            pltpu.VMEM((context, kv_width), BF16),
            pltpu.VMEM((context, kv_width), BF16),
            pltpu.VMEM((total_rows, HD), F32),
            pltpu.VMEM((total_rows, HD), F32),
            pltpu.VMEM((n, 8, HD), jnp.int32),
            pltpu.VMEM((n, total_rows, HD), BF16),
            pltpu.VMEM((n, total_rows, HD), BF16),
            pltpu.VMEM((n, 8, total_rows), F32),
            pltpu.VMEM((n, total_rows, HD), BF16),
            pltpu.VMEM((n, 8, total_rows), F32),
            pltpu.VMEM((2, 2 * steps, HD), F32),
            pltpu.SemaphoreType.DMA((7,)),
            pltpu.SemaphoreType.DMA((2,)),
            pltpu.SemaphoreType.DMA((2, n)),
            pltpu.SemaphoreType.DMA((2, n)),
            pltpu.SemaphoreType.DMA((2, n)),
            pltpu.SemaphoreType.DMA((2, n)),
            pltpu.SemaphoreType.DMA((2,)),
        ],
        compiler_params=pltpu.CompilerParams(
            collective_id=0, has_side_effects=True, vmem_limit_bytes=63 * 1024 * 1024
        ),
    )(
        lengths,
        parent_scores,
        parents,
        queries,
        new_keys,
        new_values,
        reward_weight,
        cache_keys,
        cache_values,
    )


def solution(mesh):
    beams = P(("groups", "dp"))
    split = P(("groups", "dp"), None, "tensor")
    return jax.shard_map(
        functools.partial(per_device, mesh.shape["dp"]),
        mesh=mesh,
        in_specs=(split, split, beams, beams, beams, split, split, split, P("tensor")),
        out_specs=(split, beams),
        check_vma=False,
    )
```
